32 devices in a mesh: ctx: 16 (over z, y, core), exp: 2 (over x).
Axes of the slice: x: 2, y: 2, z: 4, core: 2. Of those that a mesh axis runs over, the one named last changes fastest.
Arguments:
- residual: bfloat16 [1024, 2048], P('ctx', 'exp'), may hold values from -60 to 60
- queries: bfloat16 [1024, 512], P('ctx', 'exp'), may hold values from -6.5 to 6.5
- keys: bfloat16 [1024, 512], P('ctx', 'exp'), may hold values from -6.5 to 6.5
- values: bfloat16 [1024, 512], P('ctx', 'exp'), may hold values from -6 to 6
- out_proj: bfloat16 [512, 2048], P(None, 'exp'), may hold values from -0.5 to 0.5
- norm_gain: float32 [2048], replicated, may hold values from 0.1 to 1.9
- w_gate: bfloat16 [2, 2048, 8192], P('exp', None, 'ctx'), may hold values from -0.125 to 0.125
- w_up: bfloat16 [2, 2048, 8192], P('exp', None, 'ctx'), may hold values from -0.125 to 0.125
- w_down: bfloat16 [2, 8192, 2048], P('exp', 'ctx'), may hold values from -0.0625 to 0.0625
- routes: int32 [1024, 1], P('ctx'), may hold values from 0 to 1; in each aligned block of 64 rows (0 to 63, 64 to 127, ...) at most 32 rows name the same one
- block_mask: int32 [8, 8], replicated, may hold values from 0 to 1, as said below
Outputs:
- mixed: bfloat16 [2, 512, 2048], P('exp', 'ctx')
The draws below stay inside these ranges and needn't reach their ends.
Inputs may be any that keep to these rules, and one draw needn't show every extreme that they name: `routes`: each stored row is named by exactly 32 of the 64 rows of one index of ctx. `block_mask`: every diagonal entry is 1.
All inputs are finite; a program needn't handle non-finite values.
Results may differ from the reference program's by a relative error of at most 0.006.
Values may be sent and summed in bfloat16 or wider, within the bound.
No kernel may reach another device: no remote copies, remote signals or barrier semaphores. Data moves between devices by JAX's collectives and lax.ppermute only.
A program may use at most 64 MiB of HBM per device.

```python
import math
import jax
import jax.numpy as jnp
import numpy as np
from jax import lax

D = 2048
FF = 8192
HD = 128
BLK = 128
TOK_DEV = 64
S = 1024
HEADS = 4
EXPERTS = 2
NB = 8


def draw_queries(key, part):
    drawn = jnp.clip(1.3 * jax.random.normal(jax.random.fold_in(key, 11), (S, HEADS * HD), dtype=jnp.float32), -6.4, 6.4)
    return drawn.astype(jnp.bfloat16)


def draw_keys(key, part):
    drawn = jnp.clip(1.3 * jax.random.normal(jax.random.fold_in(key, 12), (S, HEADS * HD), dtype=jnp.float32), -6.4, 6.4)
    return drawn.astype(jnp.bfloat16)


def draw_residual(key, part):
    row_scale = jnp.exp(jax.random.uniform(jax.random.fold_in(key, 21), (S, 1), minval=-1.204, maxval=1.0986))
    col_scale = jnp.exp(jax.random.uniform(jax.random.fold_in(key, 22), (1, D), minval=-0.6931, maxval=1.6094))
    core = jnp.clip(jax.random.normal(jax.random.fold_in(key, 23), (S, D), dtype=jnp.float32), -4.0, 4.0)
    return (core * row_scale * col_scale).astype(jnp.bfloat16)


def draw_block_mask(key, part):
    modality = jax.random.randint(jax.random.fold_in(key, 31), (NB,), 0, 3)
    coin_flip = jax.random.randint(jax.random.fold_in(key, 32), (NB, NB), 0, 4)
    same_kind = modality[:, None] == modality[None, :]
    diagonal = jnp.arange(NB)[:, None] == jnp.arange(NB)[None, :]
    return jnp.where(same_kind | (coin_flip == 0) | diagonal, 1, 0).astype(jnp.int32)


def block_levels(own_key, extent, shards, least, largest):
    gain, own = 1.0, jax.random.fold_in(own_key, 6)
    for dim, blocks in shards:
        draws = jnp.exp(jax.random.uniform(jax.random.fold_in(own, dim), (blocks,), jnp.float32, least / len(shards), largest / len(shards)))
        gain = gain * jnp.repeat(draws, extent[dim] // blocks).reshape([-1 if axis == dim else 1 for axis in range(len(extent))])
    return gain


def deal_out(rng, own, number, rows, number_of, top, most, skew):
    order = jax.random.permutation(rng, number_of)
    crowded, ordinary = load_shares(number_of, rows * top, most, skew, True), load_shares(number_of, rows * top, most, skew, False)
    places = jnp.arange(number_of)

    def named(lengths, offset_by):
        used = int((lengths > 0).sum())
        fixed = max(1, used // 4)
        moved = fixed + (places - fixed + offset_by * (used - fixed)) % max(1, number_of - fixed)
        return jnp.zeros((number_of,), jnp.int32).at[order[jnp.where(places < fixed, places, moved)]].set(jnp.asarray(lengths, jnp.int32))

    lengths = jnp.where(number % 4 == 0, named(crowded, number // 4), named(ordinary, number - number // 4 - 1))
    mixed = jax.random.permutation(jax.random.fold_in(own, 3), number_of)
    source_of, taker = mixed[0:number_of // 2 * 2:2], mixed[1:number_of // 2 * 2:2]
    margin = jnp.minimum(lengths[source_of] - 1, most - lengths[taker]) // 2
    margin = jnp.where((source_of == order[0]) | (taker == order[0]) | (lengths[taker] == 0), 0, jnp.maximum(margin, 0))
    moved = jax.random.randint(jax.random.fold_in(own, 4), (number_of // 2,), 0, 1 << 20) % (margin + 1)
    lengths = lengths.at[source_of].add(-moved).at[taker].add(moved)
    items = jnp.searchsorted(jnp.cumsum(lengths), jnp.arange(rows * top), side="right").astype(jnp.int32)
    table = items.reshape(top, rows).T
    table = table[jax.random.permutation(jax.random.fold_in(own, 1), rows)]
    offset_by = jax.random.randint(jax.random.fold_in(own, 2), (rows, 1), 0, top)
    return jnp.take_along_axis(table, (jnp.arange(top)[None, :] + offset_by) % top, axis=1)


def load_shares(amount, total, reach, slope, full):
    loads = [(1 << 20) // math.isqrt(rank ** slope) + 1 for rank in range(1, amount + 1)]
    largest = reach if full else min(reach, max(-(-total // amount), total * loads[0] // sum(loads)))
    least = 1 if total - largest >= amount - 1 else 0
    counts, spare = [largest] + [least] * (amount - 1), total - largest - least * (amount - 1)
    while spare > 0:
        free = [i for i in range(1, amount) if counts[i] < largest] or [i for i in range(1, amount) if counts[i] < reach]
        whole, left = sum([loads[i] for i in free]), spare
        for i in free:
            more = min(reach - counts[i], max(1, left * loads[i] // whole), spare)
            counts[i] = counts[i] + more
            spare = spare - more
    return np.array(counts)


def centred(stream_key, dims, deviation, reach, shards=(), kind=jnp.bfloat16):
    entries = deviation * jax.random.normal(stream_key, dims, jnp.float32)
    if shards:
        entries = entries * block_levels(stream_key, dims, shards, -0.22, 0.18)
    return jnp.clip(entries, -reach, reach).astype(kind)


def setup_inputs(seed: int = 0) -> dict:
    key_of = jax.random.split(jax.random.key(seed), 12)
    residual = draw_residual(jax.random.fold_in(key_of[11], 71), 0)
    queries = draw_queries(jax.random.fold_in(key_of[11], 71), 0)
    keys = draw_keys(jax.random.fold_in(key_of[11], 71), 0)
    values = centred(key_of[3], (S, HEADS * HD), 1.0, 6.0, ((0, 16), (1, 2)))
    out_proj = centred(key_of[4], (HEADS * HD, D), HD ** -0.5, 0.5, ((1, 2),))
    norm_gain = jnp.clip(1.0 + 0.18 * jax.random.normal(key_of[5], (D,), jnp.float32), 0.1, 1.9)
    w_gate = centred(key_of[6], (EXPERTS, D, FF), D ** -0.5, 0.125, ((0, 2), (2, 16)))
    w_up = centred(key_of[7], (EXPERTS, D, FF), D ** -0.5, 0.125, ((0, 2), (2, 16)))
    w_down = centred(key_of[8], (EXPERTS, FF, D), FF ** -0.5, 0.0625, ((0, 2), (1, 16)))
    routes_keys = jax.random.split(jax.random.fold_in(key_of[9], 1), S // TOK_DEV)
    routes_turns = jax.random.permutation(jax.random.fold_in(key_of[9], 3), S // TOK_DEV)
    routes = jax.vmap(lambda own, number: deal_out(jax.random.fold_in(key_of[9], 2), own, number, TOK_DEV, EXPERTS, 1, TOK_DEV // EXPERTS, 0))(routes_keys, routes_turns).reshape((S, 1))
    block_mask = draw_block_mask(jax.random.fold_in(key_of[11], 71), 0)
    return dict(residual=residual, queries=queries, keys=keys, values=values, out_proj=out_proj, norm_gain=norm_gain, w_gate=w_gate, w_up=w_up, w_down=w_down, routes=routes, block_mask=block_mask)


def reference(residual, queries, keys, values, out_proj, norm_gain, w_gate, w_up, w_down, routes, block_mask):
    scaling = 1.0 / HD ** 0.5
    allowed = jnp.repeat(jnp.repeat(block_mask, BLK, axis=0), BLK, axis=1) > 0
    query_heads = queries.reshape(S, HEADS, HD).transpose(1, 0, 2)
    key_heads = keys.reshape(S, HEADS, HD).transpose(1, 0, 2)
    value_heads = values.reshape(S, HEADS, HD).transpose(1, 0, 2)

    def one_head(triple):
        query_h, key_h, value_h = triple
        scores = jnp.dot(query_h, key_h.T, preferred_element_type=jnp.float32) * scaling
        scores = jnp.where(allowed, scores, -1e+30)
        top_row = lax.optimization_barrier(jnp.max(scores, axis=1, keepdims=True))
        exponent = jnp.where(allowed, jnp.exp(scores - top_row), 0.0)
        totals = lax.optimization_barrier(jnp.sum(exponent, axis=1, keepdims=True))
        weights = exponent.astype(jnp.bfloat16)
        summed_v = jnp.dot(weights, value_h, preferred_element_type=jnp.float32)
        return (summed_v / totals).astype(jnp.bfloat16)
    attended = lax.map(one_head, (query_heads, key_heads, value_heads))
    attended = attended.transpose(1, 0, 2).reshape(S, HEADS * HD)
    hidden = (residual.astype(jnp.float32) + jnp.dot(attended, out_proj, preferred_element_type=jnp.float32)).astype(jnp.bfloat16)
    hidden_f = hidden.astype(jnp.float32)
    meansq = lax.optimization_barrier(jnp.mean(hidden_f * hidden_f, axis=1, keepdims=True))
    normed = (hidden_f * lax.rsqrt(meansq + 1e-05) * norm_gain).astype(jnp.bfloat16)
    position = jnp.arange(S, dtype=jnp.int32)
    target = routes[:, 0].astype(jnp.int32)
    order = jnp.argsort(target * S + position)
    chosen = order.reshape(EXPERTS, S // EXPERTS)

    def one_expert(bundle):
        picked, gate_w, up_w, down_w = bundle
        inputs = normed[picked]
        gate_v = jnp.dot(inputs, gate_w, preferred_element_type=jnp.float32)
        up_v = jnp.dot(inputs, up_w, preferred_element_type=jnp.float32)
        activ = (jax.nn.silu(gate_v) * up_v).astype(jnp.bfloat16)
        output = jnp.dot(activ, down_w, preferred_element_type=jnp.float32)
        return (hidden_f[picked] + output).astype(jnp.bfloat16)
    return lax.map(one_expert, (chosen, w_gate, w_up, w_down))
```

```python
import math

import jax
import jax.numpy as jnp
from jax import lax
from jax.sharding import PartitionSpec as P

HD = 128
BLK = 128
BF = jnp.bfloat16
F32 = jnp.float32


def dot(a, b):
    return jnp.dot(a, b, preferred_element_type=F32)


def plan(n):
    bits = [1 << k for k in range(n.bit_length() - 2, 0, -1)]
    other = bits[:-2] + bits[-2:][::-1]
    return [(a, b) for a, b in zip(bits, other)]


def offsets(stages, which):
    out = [0]
    for masks in stages:
        out = out + [o ^ masks[which] for o in out]
    return out


def body(
    residual, queries, keys, values, out_proj, norm_gain, w_gate, w_up, w_down, routes, block_mask
):
    local = residual.shape[0]
    n = lax.axis_size("ctx")
    experts = lax.axis_size("exp")
    per = local // experts
    me = lax.axis_index("ctx")
    exp_me = lax.axis_index("exp")
    core = me & 1
    stages = plan(n)
    perms = [[(i, i ^ masks[i & 1]) for i in range(n)] for masks in stages]
    width = queries.shape[1] // 2
    heads = width // HD

    def swap_core(x):
        return lax.ppermute(x, "ctx", [(i, i ^ 1) for i in range(n)])

    def swap_exp(x):
        return lax.ppermute(x, "exp", [(0, 1), (1, 0)])

    def gather(x):
        for perm in perms:
            x = jnp.concatenate([x, lax.ppermute(x, "ctx", perm)], axis=0)
        return x

    def scatter(x):
        for perm in perms[::-1]:
            half = x.shape[0] // 2
            come = lax.ppermute(x[half:].astype(BF), "ctx", perm)
            x = x[:half] + come.astype(F32)
        return x

    def mine(x):
        return lax.dynamic_slice_in_dim(x, core * width, width, axis=1)

    def others(x):
        return lax.dynamic_slice_in_dim(x, (1 - core) * width, width, axis=1)

    come = swap_core(jnp.concatenate([others(keys), others(values)], axis=1))
    both = jnp.concatenate([jnp.concatenate([mine(keys), mine(values)], axis=1), come], axis=0)
    all_kv = gather(both)

    target = routes[:, 0]
    token_ids = jnp.arange(local, dtype=jnp.int32)
    earlier = (target[:, None] == target[None, :]) & (token_ids[None, :] < token_ids[:, None])
    slot_of = target * per + jnp.sum(earlier.astype(jnp.int32), axis=1)
    placing = (slot_of[None, :] == token_ids[:, None]).astype(BF)
    q_rows = dot(placing, queries).astype(BF)
    res_rows = dot(placing, residual).astype(BF)
    q_both = jnp.concatenate([mine(q_rows), swap_core(others(q_rows))], axis=0)

    if experts == 2:
        res_own = lax.dynamic_slice_in_dim(res_rows, exp_me * per, per, axis=0)
        res_far = swap_exp(lax.dynamic_slice_in_dim(res_rows, (1 - exp_me) * per, per, axis=0))
        rows = out_proj.shape[0] // 2
        near = swap_exp(lax.dynamic_slice_in_dim(out_proj, core * rows, rows, axis=0))
        far = swap_core(near)
    else:
        res_all = lax.all_to_all(
            res_rows.reshape(experts, per, -1), "exp", split_axis=0, concat_axis=2, tiled=True
        )[0]
        proj_all = lax.all_gather(out_proj, "exp", axis=1, tiled=True)
    gate_far = swap_core(w_gate[0])
    up_far = swap_core(w_up[0])
    down_far = swap_core(w_down[0])

    off = jnp.where(
        core == 0,
        jnp.array(offsets(stages, 0), jnp.int32),
        jnp.array(offsets(stages, 1), jnp.int32),
    )
    block_ids = ((me ^ off) * local) // BLK
    blocks = block_mask.shape[0]
    mask_row = lax.dynamic_index_in_dim(block_mask, (me * local) // BLK, axis=0, keepdims=False)
    hit = (block_ids[:, None] == jnp.arange(blocks, dtype=jnp.int32)[None, :]) & (mask_row[None, :] > 0)
    allowed = jnp.repeat(jnp.any(hit, axis=1), 2 * local)[None, :]
    parts = []
    for h in range(heads):
        q_h = q_both[:, h * HD : (h + 1) * HD]
        k_h = all_kv[:, h * HD : (h + 1) * HD]
        v_h = all_kv[:, width + h * HD : width + (h + 1) * HD]
        scores = lax.dot_general(q_h, k_h, (((1,), (1,)), ((), ())), preferred_element_type=F32)
        scores = jnp.where(allowed, scores * (1.0 / math.sqrt(HD)), -1e30)
        top = jnp.max(scores, axis=1, keepdims=True)
        expo = jnp.where(allowed, jnp.exp(scores - top), 0.0)
        total = jnp.sum(expo, axis=1, keepdims=True)
        parts.append((dot(expo.astype(BF), v_h) / total).astype(BF))
    att = jnp.concatenate(parts, axis=1)
    att_far = swap_core(att[local:])
    att_near = att[:local]
    att = jnp.concatenate(
        [jnp.where(core == 0, att_near, att_far), jnp.where(core == 0, att_far, att_near)], axis=1
    )

    if experts == 2:
        first = exp_me == 0
        att_own = lax.dynamic_slice_in_dim(att, exp_me * per, per, axis=0)
        att_come = swap_exp(lax.dynamic_slice_in_dim(att, (1 - exp_me) * per, per, axis=0))
        att_all = jnp.concatenate(
            [jnp.where(first, att_own, att_come), jnp.where(first, att_come, att_own)], axis=1
        )
        near_att = lax.dynamic_slice_in_dim(att_all, core * rows, rows, axis=1)
        far_att = lax.dynamic_slice_in_dim(att_all, (1 - core) * rows, rows, axis=1)
        hid_own = (res_own.astype(F32) + dot(att_all, out_proj)).astype(BF)
        hid_far = (res_far.astype(F32) + (dot(near_att, near) + dot(far_att, far))).astype(BF)
        hidden = jnp.concatenate(
            [jnp.where(first, hid_own, hid_far), jnp.where(first, hid_far, hid_own)], axis=1
        )
    else:
        att_all = lax.all_to_all(
            att.reshape(experts, per, -1), "exp", split_axis=0, concat_axis=2, tiled=True
        )[0]
        hidden = (res_all.astype(F32) + dot(att_all, proj_all)).astype(BF)
    hidden = hidden.astype(F32)
    meansq = jnp.mean(hidden * hidden, axis=1, keepdims=True)
    normed = (hidden * lax.rsqrt(meansq + 1e-05) * norm_gain).astype(BF)

    rows_in = gather(normed)
    act_near = (jax.nn.silu(dot(rows_in, w_gate[0])) * dot(rows_in, w_up[0])).astype(BF)
    act_far = (jax.nn.silu(dot(rows_in, gate_far)) * dot(rows_in, up_far)).astype(BF)
    terms = dot(act_near, w_down[0]) + dot(act_far, down_far)
    return (hidden + scatter(terms)).astype(BF)[None]


def solution(mesh):
    in_specs = (
        P("ctx", "exp"),
        P("ctx", "exp"),
        P("ctx", "exp"),
        P("ctx", "exp"),
        P(None, "exp"),
        P(),
        P("exp", None, "ctx"),
        P("exp", None, "ctx"),
        P("exp", "ctx", None),
        P("ctx", None),
        P(),
    )
    out_specs = P("exp", "ctx", None)
    return jax.shard_map(body, mesh=mesh, in_specs=in_specs, out_specs=out_specs, check_vma=False)
```

```python
import functools
import math

import jax
import jax.numpy as jnp
from jax import lax
from jax.experimental import pallas as pl
from jax.experimental.pallas import tpu as pltpu
from jax.sharding import PartitionSpec as P

HD = 128
BLK = 128
VMEM_LIMIT = 48 * 2**20
BF = jnp.bfloat16
F32 = jnp.float32


def dot(a, b):
    return jnp.dot(a, b, preferred_element_type=F32)


def distances(bits):
    out = [0]
    for bit in bits:
        out = out + [o ^ bit for o in out]
    return out


def pairs_from(bits):
    return [bits[k : k + 2] for k in range(0, len(bits), 2)]


def gathered(stages):
    out = [0]
    for bits in stages:
        out = [o ^ d for d in distances(bits) for o in out]
    return out


def scattered(stages):
    if not stages:
        return [0]
    return [d ^ o for d in distances(stages[0]) for o in scattered(stages[1:])]


def prepare_kernel(me, mask, keys, values, queries, targets, kv, q_rows, placing, allowed, *, far):
    local, width = keys.shape
    kv[:, :width] = keys[...]
    kv[:, width:] = values[...]
    target = targets[...]
    experts = far["experts"]
    per = local // experts
    row = lax.broadcasted_iota(jnp.int32, (local, local), 0)
    col = lax.broadcasted_iota(jnp.int32, (local, local), 1)
    named = lax.broadcasted_iota(jnp.int32, (experts, local), 0) == target
    before = dot(named.astype(BF), (row < col).astype(BF))
    rank = jnp.sum(jnp.where(named, before, 0.0), axis=0, keepdims=True).astype(jnp.int32)
    place = (row == target * per + rank).astype(BF)
    placing[...] = place
    q_rows[...] = dot(place, queries[...]).astype(BF)
    block = lax.broadcasted_iota(jnp.int32, allowed.shape, 1) // local
    mine = (me[0] * local) // BLK
    chosen = jnp.zeros(allowed.shape, jnp.int32)
    for b, distance in enumerate(far["distances"]):
        chosen = jnp.where(block == b, mask[mine, ((me[0] ^ distance) * local) // BLK], chosen)
    allowed[...] = chosen


def prepare(me, mask, keys, values, queries, routes, experts, order):
    local, width = keys.shape
    smem, vmem = pl.BlockSpec(memory_space=pltpu.SMEM), pl.BlockSpec(memory_space=pltpu.VMEM)
    return pl.pallas_call(
        functools.partial(prepare_kernel, far=dict(experts=experts, distances=order)),
        out_shape=(
            jax.ShapeDtypeStruct((local, 2 * width), BF),
            jax.ShapeDtypeStruct(queries.shape, BF),
            jax.ShapeDtypeStruct((local, local), BF),
            jax.ShapeDtypeStruct((1, len(order) * local), jnp.int32),
        ),
        in_specs=[smem] * 2 + [vmem] * 4,
        out_specs=[vmem] * 4,
    )(me[None], mask, keys, values, queries, routes.reshape(1, local))


def expert_rows(x, near, far):
    total = None
    for gate, up, down in (near, far):
        act = (jax.nn.silu(dot(x, gate[...])) * dot(x, up[...])).astype(BF)
        part = dot(act, down[...])
        total = part if total is None else total + part
    return total


def expert_kernel(
    att_at, res_at, att, res_hbm, proj_hbm, gain, gate0, up0, down0, gate1, up1, down1,
    own, keep, send, att_rows, hidden, normed, res, proj, gates, ups, downs, sems,
):
    blocks, per, feats = res.shape
    sources, _, width = att.shape
    sources //= blocks
    pieces = send.shape[0] + 1
    size = blocks * per // pieces
    rows = 2 * size
    tile = math.gcd(feats, 512)
    cols = [slice(c, c + tile) for c in range(0, feats, tile)]
    moves = [
        pltpu.make_async_copy(src, dst, sems.at[i])
        for i, (src, dst) in enumerate(
            (
                (proj_hbm, proj), (res_hbm, res), (gate0, gates.at[0]), (up0, ups.at[0]),
                (gate1, gates.at[1]), (up1, ups.at[1]), (down0, downs.at[0]), (down1, downs.at[1]),
            )
        )
    ]
    for move in moves:
        move.start()
    for b in range(blocks):
        for s in range(sources):
            att_rows[b * per : (b + 1) * per, s * width : (s + 1) * width] = att[
                att_at[b] * sources + s
            ]
    moves[0].wait()
    moves[1].wait()
    spans = [slice(k, k + rows) for k in range(0, blocks * per, rows)]
    for span in spans:
        squares = 0.0
        for c in cols:
            projected = dot(att_rows[span, :], proj[:, c])
            added = jnp.concatenate(
                [res[res_at[b], :, c] for b in range(span.start // per, span.stop // per)], axis=0
            )
            part = (added.astype(F32) + projected).astype(BF)
            hidden[span, c] = part
            part = part.astype(F32)
            squares = squares + jnp.sum(part * part, axis=1, keepdims=True)
        scale = lax.rsqrt(squares / feats + 1e-05)
        for c in cols:
            normed[span, c] = (hidden[span, c].astype(F32) * scale * gain[:, c]).astype(BF)
    own[...] = hidden[:per, :].astype(F32)
    acts = []
    for side in (0, 1):
        moves[2 + 2 * side].wait()
        moves[3 + 2 * side].wait()
        for span in spans:
            x = normed[span, :]
            acts.append((jax.nn.silu(dot(x, gates[side])) * dot(x, ups[side])).astype(BF))
    moves[6].wait()
    moves[7].wait()
    for k in range(len(spans)):
        for c in cols:
            total = dot(acts[k], downs[0, :, c]) + dot(acts[len(spans) + k], downs[1, :, c])
            for piece in (0, 1):
                part = total[piece * size : (piece + 1) * size]
                if 2 * k + piece == 0:
                    keep[:, c] = part
                else:
                    send[2 * k + piece - 1, :, c] = part.astype(BF)


def expert(att_at, res_at, att, res, proj, gain, near, far):
    blocks, per, feats = res.shape
    units = near[0].shape[1]
    rows = blocks * per
    smem, vmem = pl.BlockSpec(memory_space=pltpu.SMEM), pl.BlockSpec(memory_space=pltpu.VMEM)
    hbm = pl.BlockSpec(memory_space=pl.ANY)
    return pl.pallas_call(
        expert_kernel,
        out_shape=(
            jax.ShapeDtypeStruct((per, feats), F32),
            jax.ShapeDtypeStruct((rows // 4, feats), F32),
            jax.ShapeDtypeStruct((3, rows // 4, feats), BF),
        ),
        in_specs=[smem] * 2 + [vmem] + [hbm] * 2 + [vmem] + [hbm] * 6,
        out_specs=[vmem] * 3,
        scratch_shapes=[
            pltpu.VMEM((rows, proj.shape[0]), BF),
            pltpu.VMEM((rows, feats), BF),
            pltpu.VMEM((rows, feats), BF),
            pltpu.VMEM(res.shape, BF),
            pltpu.VMEM(proj.shape, BF),
            pltpu.VMEM((2, feats, units), BF),
            pltpu.VMEM((2, feats, units), BF),
            pltpu.VMEM((2, units, feats), BF),
            pltpu.SemaphoreType.DMA((8,)),
        ],
        compiler_params=pltpu.CompilerParams(vmem_limit_bytes=VMEM_LIMIT),
        cost_estimate=pl.CostEstimate(
            flops=12 * rows * feats * units, bytes_accessed=12 * feats * units, transcendentals=0
        ),
    )(att_at, res_at, att, res, proj, gain[None], *near, *far)


def body(
    residual, queries, keys, values, out_proj, norm_gain, w_gate, w_up, w_down, routes, block_mask
):
    local = residual.shape[0]
    n = lax.axis_size("ctx")
    experts = lax.axis_size("exp")
    per = local // experts
    me = lax.axis_index("ctx")
    exp_me = lax.axis_index("exp")
    core = me & 1
    bits = [1 << k for k in range(1, n.bit_length() - 1)]
    kv_stages = [pair[::-1] for pair in pairs_from(bits[::-1])]
    sum_stages = pairs_from(bits)
    one, two = bits[::-1], bits[:1:-1] + bits[:2]
    res_masks = list(zip(one, two))

    def by_core(even, odd):
        return jnp.where(core == 0, even, odd)

    def move(x, even, odd=None):
        masks = (even, even if odd is None else odd)
        return lax.ppermute(x, "ctx", [(i, i ^ masks[i & 1]) for i in range(n)])

    def swap_core(x):
        return move(x, 1)

    def swap_exp(x):
        return lax.ppermute(x, "exp", [(0, 1), (1, 0)])

    def gather(x, stages):
        for bits in stages:
            x = jnp.concatenate([x] + [move(x, d) for d in distances(bits)[1:]], axis=0)
        return x

    def scatter(keep, send):
        for k, stage in enumerate(sum_stages):
            if k:
                pieces = jnp.split(keep, 1 << len(stage), axis=0)
                keep, send = pieces[0], [piece.astype(BF) for piece in pieces[1:]]
            for piece, distance in zip(send, distances(stage)[1:]):
                keep = keep + move(piece, distance).astype(F32)
        return keep

    kv_order = gathered(kv_stages)
    width = keys.shape[1]
    heads = width // HD
    all_kv, q_rows, placing, allowed = prepare(
        me, block_mask, keys, values, queries, routes, experts, kv_order + [o ^ 1 for o in kv_order]
    )
    allowed = allowed > 0
    all_kv = gather(all_kv, kv_stages[:1])
    rows = out_proj.shape[0] // 2
    proj_go = lax.dynamic_slice_in_dim(out_proj, core * rows, rows, axis=0)
    all_kv, proj_go = lax.optimization_barrier((all_kv, proj_go))
    all_kv = gather(all_kv, kv_stages[1:-1])
    last = [move(x, d) for d in distances(kv_stages[-1])[1:] for x in jnp.split(all_kv, 2, axis=0)]
    all_kv = jnp.concatenate([all_kv] + last, axis=0)
    far_kv = swap_core(all_kv)

    near_w = (w_gate[0], w_up[0], w_down[0])
    far_w = tuple(swap_core(w) for w in near_w)
    direct = experts == 2 and per % 32 == 0
    if direct:
        first = exp_me == 0

        def both_halves(mine, theirs):
            return jnp.concatenate(
                [jnp.where(first, mine, theirs), jnp.where(first, theirs, mine)], axis=1
            )

        own_rows = lax.dynamic_slice_in_dim(placing, exp_me * per, per, axis=0)
        res_both = both_halves(residual, swap_exp(residual))
        res_all = dot(own_rows, res_both).astype(BF)
        for masks in res_masks:
            res_all = jnp.concatenate([res_all, move(res_all, *masks)], axis=0)
        proj_near = swap_exp(proj_go)
        proj_far = swap_core(proj_near)
        proj_come = jnp.concatenate([by_core(proj_near, proj_far), by_core(proj_far, proj_near)], axis=0)
        proj_all = both_halves(out_proj, proj_come)
    else:
        res_rows = dot(placing, residual).astype(BF)
        res_all = lax.all_to_all(
            res_rows.reshape(experts, per, -1), "exp", split_axis=0, concat_axis=2, tiled=True
        )[0]
        proj_all = lax.all_gather(out_proj, "exp", axis=1, tiled=True)

    all_kv = jnp.concatenate([all_kv, far_kv], axis=0)
    parts = []
    for h in range(heads):
        cols = slice(h * HD, (h + 1) * HD)
        k_h, v_h = all_kv[:, :width][:, cols], all_kv[:, width:][:, cols]
        scores = lax.dot_general(
            q_rows[:, cols], k_h, (((1,), (1,)), ((), ())), preferred_element_type=F32
        )
        scores = jnp.where(allowed, scores * (1.0 / math.sqrt(HD)), -1e30)
        top = jnp.max(scores, axis=1, keepdims=True)
        expo = jnp.where(allowed, jnp.exp(scores - top), 0.0)
        total = jnp.sum(expo, axis=1, keepdims=True)
        parts.append((dot(expo.astype(BF), v_h) / total).astype(BF))
    att = jnp.concatenate(parts, axis=1).reshape(experts, per, width)

    if direct:
        groups = [[(2 * k + c) * experts + e for k in range(n // 2) for e in range(experts)] for c in (0, 1)]
        go = jnp.broadcast_to(att[None], (n // 2, experts, per, width)).reshape(-1, per, width)
        att_all = lax.all_to_all(
            go, ("ctx", "exp"), split_axis=0, concat_axis=0, axis_index_groups=groups, tiled=True
        )
        order = scattered(sum_stages)
        places = [gathered([[masks[c]] for masks in res_masks]) for c in (0, 1)]
        res_at = by_core(*(jnp.array([place.index(o) for o in order], jnp.int32) for place in places))
        hidden, keep, send = expert(
            (me ^ jnp.array(order, jnp.int32)) >> 1, res_at, att_all,
            res_all.reshape(n // 2, per, -1), proj_all, norm_gain, near_w, far_w,
        )
        summed = scatter(keep, [send[k] for k in range(3)])
    else:
        att_all = lax.all_to_all(att, "exp", split_axis=0, concat_axis=2, tiled=True)[0]
        hidden = (res_all.astype(F32) + dot(att_all, proj_all)).astype(BF).astype(F32)
        meansq = jnp.mean(hidden * hidden, axis=1, keepdims=True)
        normed = (hidden * lax.rsqrt(meansq + 1e-05) * norm_gain).astype(BF)
        order = scattered(sum_stages)
        found = gather(normed, sum_stages).reshape(n // 2, per, -1)
        found = jnp.stack([found[gathered(sum_stages).index(o)] for o in order]).reshape(n // 2 * per, -1)
        pieces = jnp.split(expert_rows(found, near_w, far_w), 4, axis=0)
        summed = scatter(pieces[0], [piece.astype(BF) for piece in pieces[1:]])
    return (hidden + summed).astype(BF)[None]


def solution(mesh):
    in_specs = (
        P("ctx", "exp"),
        P("ctx", "exp"),
        P("ctx", "exp"),
        P("ctx", "exp"),
        P(None, "exp"),
        P(),
        P("exp", None, "ctx"),
        P("exp", None, "ctx"),
        P("exp", "ctx", None),
        P("ctx", None),
        P(),
    )
    out_specs = P("exp", "ctx", None)
    return jax.shard_map(body, mesh=mesh, in_specs=in_specs, out_specs=out_specs, check_vma=False)
```

```python
import functools
import math

import jax
import jax.numpy as jnp
from jax import lax
from jax.experimental import pallas as pl
from jax.experimental.pallas import tpu as pltpu
from jax.sharding import PartitionSpec as P

HD = 128
BLK = 128
VMEM_LIMIT = 48 * 2**20
BF = jnp.bfloat16
F32 = jnp.float32


def dot(a, b):
    return jnp.dot(a, b, preferred_element_type=F32)


def distances(bits):
    out = [0]
    for bit in bits:
        out = out + [o ^ bit for o in out]
    return out


def pairs_from(bits):
    return [bits[k : k + 2] for k in range(0, len(bits), 2)]


def gathered(stages):
    out = [0]
    for bits in stages:
        out = [o ^ d for d in distances(bits) for o in out]
    return out


def scattered(stages):
    if not stages:
        return [0]
    return [d ^ o for d in distances(stages[0]) for o in scattered(stages[1:])]


def prepare_kernel(me, mask, keys, values, queries, targets, kv, q_rows, placing, allowed, *, far):
    local, width = keys.shape
    kv[:, :width] = keys[...]
    kv[:, width:] = values[...]
    target = targets[...]
    experts = far["experts"]
    per = local // experts
    row = lax.broadcasted_iota(jnp.int32, (local, local), 0)
    col = lax.broadcasted_iota(jnp.int32, (local, local), 1)
    named = lax.broadcasted_iota(jnp.int32, (experts, local), 0) == target
    before = dot(named.astype(BF), (row < col).astype(BF))
    rank = jnp.sum(jnp.where(named, before, 0.0), axis=0, keepdims=True).astype(jnp.int32)
    place = (row == target * per + rank).astype(BF)
    placing[...] = place
    q_rows[...] = dot(place, queries[...]).astype(BF)
    block = lax.broadcasted_iota(jnp.int32, allowed.shape, 1) // local
    mine = (me[0] * local) // BLK
    chosen = jnp.zeros(allowed.shape, jnp.int32)
    for b, distance in enumerate(far["distances"]):
        chosen = jnp.where(block == b, mask[mine, ((me[0] ^ distance) * local) // BLK], chosen)
    allowed[...] = chosen


def prepare(me, mask, keys, values, queries, routes, experts, order):
    local, width = keys.shape
    smem, vmem = pl.BlockSpec(memory_space=pltpu.SMEM), pl.BlockSpec(memory_space=pltpu.VMEM)
    return pl.pallas_call(
        functools.partial(prepare_kernel, far=dict(experts=experts, distances=order)),
        out_shape=(
            jax.ShapeDtypeStruct((local, 2 * width), BF),
            jax.ShapeDtypeStruct(queries.shape, BF),
            jax.ShapeDtypeStruct((local, local), BF),
            jax.ShapeDtypeStruct((1, len(order) * local), jnp.int32),
        ),
        in_specs=[smem] * 2 + [vmem] * 4,
        out_specs=[vmem] * 4,
    )(me[None], mask, keys, values, queries, routes.reshape(1, local))


def expert_rows(x, near, far):
    total = None
    for gate, up, down in (near, far):
        act = (jax.nn.silu(dot(x, gate[...])) * dot(x, up[...])).astype(BF)
        part = dot(act, down[...])
        total = part if total is None else total + part
    return total


def expert_kernel(
    att_at, res_at, att, res_hbm, proj_hbm, gain, gate0, up0, down0, gate1, up1, down1,
    own, keep, send, att_rows, hidden, normed, res, proj, gates, ups, downs, sems,
):
    blocks, per, feats = res.shape
    sources, _, width = att.shape
    sources //= blocks
    pieces = send.shape[0] + 1
    size = blocks * per // pieces
    rows = 2 * size
    tile = math.gcd(feats, 512)
    cols = [slice(c, c + tile) for c in range(0, feats, tile)]
    moves = [
        pltpu.make_async_copy(src, dst, sems.at[i])
        for i, (src, dst) in enumerate(
            (
                (proj_hbm, proj), (res_hbm, res), (gate0, gates.at[0]), (up0, ups.at[0]),
                (gate1, gates.at[1]), (up1, ups.at[1]), (down0, downs.at[0]), (down1, downs.at[1]),
            )
        )
    ]
    for move in moves:
        move.start()
    for b in range(blocks):
        for s in range(sources):
            att_rows[b * per : (b + 1) * per, s * width : (s + 1) * width] = att[
                att_at[b] * sources + s
            ]
    moves[0].wait()
    moves[1].wait()
    spans = [slice(k, k + rows) for k in range(0, blocks * per, rows)]
    for span in spans:
        squares = 0.0
        for c in cols:
            projected = dot(att_rows[span, :], proj[:, c])
            added = jnp.concatenate(
                [res[res_at[b], :, c] for b in range(span.start // per, span.stop // per)], axis=0
            )
            part = (added.astype(F32) + projected).astype(BF)
            hidden[span, c] = part
            part = part.astype(F32)
            squares = squares + jnp.sum(part * part, axis=1, keepdims=True)
        scale = lax.rsqrt(squares / feats + 1e-05)
        for c in cols:
            normed[span, c] = (hidden[span, c].astype(F32) * scale * gain[:, c]).astype(BF)
    own[...] = hidden[:per, :].astype(F32)
    acts = []
    for side in (0, 1):
        moves[2 + 2 * side].wait()
        moves[3 + 2 * side].wait()
        for span in spans:
            x = normed[span, :]
            acts.append((jax.nn.silu(dot(x, gates[side])) * dot(x, ups[side])).astype(BF))
    moves[6].wait()
    moves[7].wait()
    for k in range(len(spans)):
        for c in cols:
            total = dot(acts[k], downs[0, :, c]) + dot(acts[len(spans) + k], downs[1, :, c])
            for piece in (0, 1):
                part = total[piece * size : (piece + 1) * size]
                if 2 * k + piece == 0:
                    keep[:, c] = part
                else:
                    send[2 * k + piece - 1, :, c] = part.astype(BF)


def expert(att_at, res_at, att, res, proj, gain, near, far):
    blocks, per, feats = res.shape
    units = near[0].shape[1]
    rows = blocks * per
    smem, vmem = pl.BlockSpec(memory_space=pltpu.SMEM), pl.BlockSpec(memory_space=pltpu.VMEM)
    hbm = pl.BlockSpec(memory_space=pl.ANY)
    return pl.pallas_call(
        expert_kernel,
        out_shape=(
            jax.ShapeDtypeStruct((per, feats), F32),
            jax.ShapeDtypeStruct((rows // 4, feats), F32),
            jax.ShapeDtypeStruct((3, rows // 4, feats), BF),
        ),
        in_specs=[smem] * 2 + [vmem] + [hbm] * 2 + [vmem] + [hbm] * 6,
        out_specs=[vmem] * 3,
        scratch_shapes=[
            pltpu.VMEM((rows, proj.shape[0]), BF),
            pltpu.VMEM((rows, feats), BF),
            pltpu.VMEM((rows, feats), BF),
            pltpu.VMEM(res.shape, BF),
            pltpu.VMEM(proj.shape, BF),
            pltpu.VMEM((2, feats, units), BF),
            pltpu.VMEM((2, feats, units), BF),
            pltpu.VMEM((2, units, feats), BF),
            pltpu.SemaphoreType.DMA((8,)),
        ],
        compiler_params=pltpu.CompilerParams(vmem_limit_bytes=VMEM_LIMIT),
        cost_estimate=pl.CostEstimate(
            flops=12 * rows * feats * units, bytes_accessed=12 * feats * units, transcendentals=0
        ),
    )(att_at, res_at, att, res, proj, gain[None], *near, *far)


def body(
    residual, queries, keys, values, out_proj, norm_gain, w_gate, w_up, w_down, routes, block_mask
):
    local = residual.shape[0]
    n = lax.axis_size("ctx")
    experts = lax.axis_size("exp")
    per = local // experts
    me = lax.axis_index("ctx")
    exp_me = lax.axis_index("exp")
    core = me & 1
    bits = [1 << k for k in range(1, n.bit_length() - 1)]
    kv_stages = [pair[::-1] for pair in pairs_from(bits[::-1])]
    sum_stages = pairs_from(bits)
    one, two = bits[::-1], bits[:1:-1] + bits[:2]
    res_masks = list(zip(one, two))

    def by_core(even, odd):
        return jnp.where(core == 0, even, odd)

    def move(x, even, odd=None):
        masks = (even, even if odd is None else odd)
        return lax.ppermute(x, "ctx", [(i, i ^ masks[i & 1]) for i in range(n)])

    def swap_core(x):
        return move(x, 1)

    def swap_exp(x):
        return lax.ppermute(x, "exp", [(0, 1), (1, 0)])

    def gather(x, stages):
        for bits in stages:
            x = jnp.concatenate([x] + [move(x, d) for d in distances(bits)[1:]], axis=0)
        return x

    def scatter(keep, send, stages):
        parts = 1 << len(stages[1]) if len(stages) > 1 else 1
        sums = []
        for part in reversed(range(parts)):
            total = jnp.split(keep, parts, axis=0)[part]
            for piece, distance in reversed(list(zip(send, distances(stages[0])[1:]))):
                total = total + move(jnp.split(piece, parts, axis=0)[part], distance).astype(F32)
            sums.insert(0, total)
        if parts == 1:
            return sums[0]
        return scatter(sums[0], [total.astype(BF) for total in sums[1:]], stages[1:])

    kv_order = gathered(kv_stages)
    width = keys.shape[1]
    heads = width // HD
    all_kv, q_rows, placing, allowed = prepare(
        me, block_mask, keys, values, queries, routes, experts, kv_order + [o ^ 1 for o in kv_order]
    )
    allowed = allowed > 0
    rows = out_proj.shape[0] // 2
    proj_go = lax.dynamic_slice_in_dim(out_proj, core * rows, rows, axis=0)
    all_kv = gather(all_kv, kv_stages[:1])
    if experts == 2:
        all_kv, res_come = lax.optimization_barrier((all_kv, swap_exp(residual)))
    all_kv = gather(all_kv, kv_stages[1:-1])
    last = [move(x, d) for d in distances(kv_stages[-1])[1:] for x in jnp.split(all_kv, 2, axis=0)]
    all_kv = jnp.concatenate([all_kv] + last, axis=0)
    far_kv = swap_core(all_kv)

    near_w = (w_gate[0], w_up[0], w_down[0])
    direct = experts == 2 and per % 32 == 0
    if direct:
        first = exp_me == 0

        def both_halves(mine, theirs):
            return jnp.concatenate(
                [jnp.where(first, mine, theirs), jnp.where(first, theirs, mine)], axis=1
            )

        own_rows = lax.dynamic_slice_in_dim(placing, exp_me * per, per, axis=0)
        res_both = both_halves(residual, res_come)
        res_all = dot(own_rows, res_both).astype(BF)
        res_all = jnp.concatenate([res_all, move(res_all, *res_masks[0])], axis=0)
        proj_near = swap_exp(proj_go)
    else:
        res_rows = dot(placing, residual).astype(BF)
        res_all = lax.all_to_all(
            res_rows.reshape(experts, per, -1), "exp", split_axis=0, concat_axis=2, tiled=True
        )[0]
        proj_all = lax.all_gather(out_proj, "exp", axis=1, tiled=True)

    all_kv = jnp.concatenate([all_kv, far_kv], axis=0)
    parts = []
    for h in range(heads):
        cols = slice(h * HD, (h + 1) * HD)
        k_h, v_h = all_kv[:, :width][:, cols], all_kv[:, width:][:, cols]
        scores = lax.dot_general(
            q_rows[:, cols], k_h, (((1,), (1,)), ((), ())), preferred_element_type=F32
        )
        scores = jnp.where(allowed, scores * (1.0 / math.sqrt(HD)), -1e30)
        top = jnp.max(scores, axis=1, keepdims=True)
        expo = jnp.where(allowed, jnp.exp(scores - top), 0.0)
        total = jnp.sum(expo, axis=1, keepdims=True)
        parts.append((dot(expo.astype(BF), v_h) / total).astype(BF))
    att = jnp.concatenate(parts, axis=1).reshape(experts, per, width)

    if direct:
        att, res_all = lax.optimization_barrier((att, res_all))
        go = jnp.broadcast_to(att[None], (n // 2, experts, per, width)).reshape(-1, per, width)
        go, go_w, proj_near = lax.optimization_barrier((go, near_w, proj_near))
        proj_far = swap_core(proj_near)
        proj_come = jnp.concatenate([by_core(proj_near, proj_far), by_core(proj_far, proj_near)], axis=0)
        proj_all = both_halves(out_proj, proj_come)
        far_w = tuple(swap_core(w) for w in go_w)
        for masks in res_masks[1:]:
            res_all = jnp.concatenate([res_all, move(res_all, *masks)], axis=0)
        groups = [[(2 * k + c) * experts + e for k in range(n // 2) for e in range(experts)] for c in (0, 1)]
        att_all = lax.all_to_all(
            go, ("ctx", "exp"), split_axis=0, concat_axis=0, axis_index_groups=groups, tiled=True
        )
        order = scattered(sum_stages)
        places = [gathered([[masks[c]] for masks in res_masks]) for c in (0, 1)]
        res_at = by_core(*(jnp.array([place.index(o) for o in order], jnp.int32) for place in places))
        hidden, keep, send = expert(
            (me ^ jnp.array(order, jnp.int32)) >> 1, res_at, att_all,
            res_all.reshape(n // 2, per, -1), proj_all, norm_gain, near_w, far_w,
        )
        summed = scatter(keep, [send[k] for k in range(3)], sum_stages)
    else:
        att_all = lax.all_to_all(att, "exp", split_axis=0, concat_axis=2, tiled=True)[0]
        hidden = (res_all.astype(F32) + dot(att_all, proj_all)).astype(BF).astype(F32)
        meansq = jnp.mean(hidden * hidden, axis=1, keepdims=True)
        normed = (hidden * lax.rsqrt(meansq + 1e-05) * norm_gain).astype(BF)
        order = scattered(sum_stages)
        far_w = tuple(swap_core(w) for w in near_w)
        found = gather(normed, sum_stages).reshape(n // 2, per, -1)
        found = jnp.stack([found[gathered(sum_stages).index(o)] for o in order]).reshape(n // 2 * per, -1)
        pieces = jnp.split(expert_rows(found, near_w, far_w), 4, axis=0)
        summed = scatter(pieces[0], [piece.astype(BF) for piece in pieces[1:]], sum_stages)
    return (hidden + summed).astype(BF)[None]


def solution(mesh):
    in_specs = (
        P("ctx", "exp"),
        P("ctx", "exp"),
        P("ctx", "exp"),
        P("ctx", "exp"),
        P(None, "exp"),
        P(),
        P("exp", None, "ctx"),
        P("exp", None, "ctx"),
        P("exp", "ctx", None),
        P("ctx", None),
        P(),
    )
    out_specs = P("exp", "ctx", None)
    return jax.shard_map(body, mesh=mesh, in_specs=in_specs, out_specs=out_specs, check_vma=False)
```

```python
import functools
import math

import jax
import jax.numpy as jnp
from jax import lax
from jax.experimental import pallas as pl
from jax.experimental.pallas import tpu as pltpu
from jax.sharding import PartitionSpec as P

HD = 128
BLK = 128
VMEM_LIMIT = 48 * 2**20
BF = jnp.bfloat16
F32 = jnp.float32


def dot(a, b):
    return jnp.dot(a, b, preferred_element_type=F32)


def distances(bits):
    out = [0]
    for bit in bits:
        out = out + [o ^ bit for o in out]
    return out


def pairs_from(bits):
    return [bits[k : k + 2] for k in range(0, len(bits), 2)]


def gathered(stages):
    out = [0]
    for bits in stages:
        out = [o ^ d for d in distances(bits) for o in out]
    return out


def scattered(stages):
    if not stages:
        return [0]
    return [d ^ o for d in distances(stages[0]) for o in scattered(stages[1:])]


def prepare_kernel(me, mask, keys, values, queries, targets, kv, q_rows, placing, allowed, *, far):
    local, width = keys.shape
    kv[:, :width] = keys[...]
    kv[:, width:] = values[...]
    target = targets[...]
    experts = far["experts"]
    per = local // experts
    row = lax.broadcasted_iota(jnp.int32, (local, local), 0)
    col = lax.broadcasted_iota(jnp.int32, (local, local), 1)
    named = lax.broadcasted_iota(jnp.int32, (experts, local), 0) == target
    before = dot(named.astype(BF), (row < col).astype(BF))
    rank = jnp.sum(jnp.where(named, before, 0.0), axis=0, keepdims=True).astype(jnp.int32)
    place = (row == target * per + rank).astype(BF)
    placing[...] = place
    q_rows[...] = dot(place, queries[...]).astype(BF)
    block = lax.broadcasted_iota(jnp.int32, allowed.shape, 1) // local
    mine = (me[0] * local) // BLK
    chosen = jnp.zeros(allowed.shape, jnp.int32)
    for b, distance in enumerate(far["distances"]):
        chosen = jnp.where(block == b, mask[mine, ((me[0] ^ distance) * local) // BLK], chosen)
    allowed[...] = chosen


def prepare(me, mask, keys, values, queries, routes, experts, order):
    local, width = keys.shape
    smem, vmem = pl.BlockSpec(memory_space=pltpu.SMEM), pl.BlockSpec(memory_space=pltpu.VMEM)
    return pl.pallas_call(
        functools.partial(prepare_kernel, far=dict(experts=experts, distances=order)),
        out_shape=(
            jax.ShapeDtypeStruct((local, 2 * width), BF),
            jax.ShapeDtypeStruct(queries.shape, BF),
            jax.ShapeDtypeStruct((local, local), BF),
            jax.ShapeDtypeStruct((1, len(order) * local), jnp.int32),
        ),
        in_specs=[smem] * 2 + [vmem] * 4,
        out_specs=[vmem] * 4,
    )(me[None], mask, keys, values, queries, routes.reshape(1, local))


def expert_rows(x, near, far):
    total = None
    for gate, up, down in (near, far):
        act = (jax.nn.silu(dot(x, gate[...])) * dot(x, up[...])).astype(BF)
        part = dot(act, down[...])
        total = part if total is None else total + part
    return total


def expert_kernel(
    att_at, res_at, att, res0, res1, res2, res3, proj, gain, gate0, up0, down0, gate1, up1, down1,
    own, keep, send, att_rows, hidden, normed, res, gates, ups, downs, sems,
):
    blocks, per, feats = res.shape
    sources, _, width = att.shape
    sources //= blocks
    pieces = send.shape[0] + 1
    size = blocks * per // pieces
    rows = 2 * size
    tile = math.gcd(feats, 512)
    cols = [slice(c, c + tile) for c in range(0, feats, tile)]
    moves = [
        pltpu.make_async_copy(src, dst, sems.at[i])
        for i, (src, dst) in enumerate(
            (
                (gate0, gates.at[0]), (up0, ups.at[0]),
                (gate1, gates.at[1]), (up1, ups.at[1]), (down0, downs.at[0]), (down1, downs.at[1]),
                (res0, res.at[: blocks // 4]), (res1, res.at[blocks // 4 : blocks // 2]),
                (res2, res.at[blocks // 2 : 3 * blocks // 4]), (res3, res.at[3 * blocks // 4 :]),
            )
        )
    ]
    for k in (6, 7, 8, 9, 0, 1, 2, 3, 4, 5):
        moves[k].start()
    for b in range(blocks):
        for s in range(sources):
            att_rows[b * per : (b + 1) * per, s * width : (s + 1) * width] = att[
                att_at[b] * sources + s
            ]
    for k in (6, 7, 8, 9):
        moves[k].wait()
    spans = [slice(k, k + rows) for k in range(0, blocks * per, rows)]
    for span in spans:
        squares = 0.0
        for c in cols:
            projected = dot(att_rows[span, :], proj[:, c])
            added = jnp.concatenate(
                [res[res_at[b], :, c] for b in range(span.start // per, span.stop // per)], axis=0
            )
            part = (added.astype(F32) + projected).astype(BF)
            hidden[span, c] = part
            part = part.astype(F32)
            squares = squares + jnp.sum(part * part, axis=1, keepdims=True)
        scale = lax.rsqrt(squares / feats + 1e-05)
        for c in cols:
            normed[span, c] = (hidden[span, c].astype(F32) * scale * gain[:, c]).astype(BF)
    own[...] = hidden[:per, :].astype(F32)
    acts = []
    for side in (0, 1):
        moves[2 * side].wait()
        moves[2 * side + 1].wait()
        for span in spans:
            x = normed[span, :]
            acts.append((jax.nn.silu(dot(x, gates[side])) * dot(x, ups[side])).astype(BF))
    moves[4].wait()
    moves[5].wait()
    for k in range(len(spans)):
        for c in cols:
            total = dot(acts[k], downs[0, :, c]) + dot(acts[len(spans) + k], downs[1, :, c])
            for piece in (0, 1):
                part = total[piece * size : (piece + 1) * size]
                if 2 * k + piece == 0:
                    keep[:, c] = part
                else:
                    send[2 * k + piece - 1, :, c] = part.astype(BF)


def expert(att_at, res_at, att, res, proj, gain, near, far):
    quarter, per, feats = res[0].shape
    blocks = 4 * quarter
    units = near[0].shape[1]
    rows = blocks * per
    smem, vmem = pl.BlockSpec(memory_space=pltpu.SMEM), pl.BlockSpec(memory_space=pltpu.VMEM)
    hbm = pl.BlockSpec(memory_space=pl.ANY)
    return pl.pallas_call(
        expert_kernel,
        out_shape=(
            jax.ShapeDtypeStruct((per, feats), F32),
            jax.ShapeDtypeStruct((rows // 4, feats), F32),
            jax.ShapeDtypeStruct((3, rows // 4, feats), BF),
        ),
        in_specs=[smem] * 2 + [vmem] + [hbm] * 4 + [vmem] * 2 + [hbm] * 6,
        out_specs=[vmem] * 3,
        scratch_shapes=[
            pltpu.VMEM((rows, proj.shape[0]), BF),
            pltpu.VMEM((rows, feats), BF),
            pltpu.VMEM((rows, feats), BF),
            pltpu.VMEM((blocks, per, feats), BF),
            pltpu.VMEM((2, feats, units), BF),
            pltpu.VMEM((2, feats, units), BF),
            pltpu.VMEM((2, units, feats), BF),
            pltpu.SemaphoreType.DMA((10,)),
        ],
        compiler_params=pltpu.CompilerParams(vmem_limit_bytes=VMEM_LIMIT),
        cost_estimate=pl.CostEstimate(
            flops=12 * rows * feats * units, bytes_accessed=12 * feats * units, transcendentals=0
        ),
    )(att_at, res_at, att, *res, proj, gain[None], *near, *far)


def body(
    residual, queries, keys, values, out_proj, norm_gain, w_gate, w_up, w_down, routes, block_mask
):
    local = residual.shape[0]
    n = lax.axis_size("ctx")
    experts = lax.axis_size("exp")
    per = local // experts
    me = lax.axis_index("ctx")
    exp_me = lax.axis_index("exp")
    core = me & 1
    bits = [1 << k for k in range(1, n.bit_length() - 1)]
    kv_stages = [pair[::-1] for pair in pairs_from(bits[::-1])]
    sum_stages = pairs_from(bits)
    one, two = bits[::-1], bits[:1:-1] + bits[:2]
    res_masks = list(zip(one, two))

    def by_core(even, odd):
        return jnp.where(core == 0, even, odd)

    def move(x, even, odd=None):
        masks = (even, even if odd is None else odd)
        return lax.ppermute(x, "ctx", [(i, i ^ masks[i & 1]) for i in range(n)])

    def swap_core(x):
        return move(x, 1)

    def swap_exp(x):
        return lax.ppermute(x, "exp", [(0, 1), (1, 0)])

    def gather(x, stages):
        for bits in stages:
            x = jnp.concatenate([x] + [move(x, d) for d in distances(bits)[1:]], axis=0)
        return x

    def scatter(keep, send, stages):
        parts = 1 << len(stages[1]) if len(stages) > 1 else 1
        sums = []
        for part in reversed(range(parts)):
            total = jnp.split(keep, parts, axis=0)[part]
            for piece, distance in reversed(list(zip(send, distances(stages[0])[1:]))):
                total = total + move(jnp.split(piece, parts, axis=0)[part], distance).astype(F32)
            sums.insert(0, total)
        if parts == 1:
            return sums[0]
        return scatter(sums[0], [total.astype(BF) for total in sums[1:]], stages[1:])

    kv_order = gathered(kv_stages)
    width = keys.shape[1]
    heads = width // HD
    all_kv, q_rows, placing, allowed = prepare(
        me, block_mask, keys, values, queries, routes, experts, kv_order + [o ^ 1 for o in kv_order]
    )
    allowed = allowed > 0
    rows = out_proj.shape[0] // 2
    proj_go = lax.dynamic_slice_in_dim(out_proj, core * rows, rows, axis=0)
    all_kv = gather(all_kv, kv_stages[:1])
    if experts == 2:
        all_kv, res_come = lax.optimization_barrier((all_kv, swap_exp(residual)))
    all_kv = gather(all_kv, kv_stages[1:-1])
    last = [move(x, d) for d in distances(kv_stages[-1])[1:] for x in jnp.split(all_kv, 2, axis=0)]
    all_kv = jnp.concatenate([all_kv] + last, axis=0)
    far_kv = swap_core(all_kv)

    near_w = (w_gate[0], w_up[0], w_down[0])
    direct = experts == 2 and per % 32 == 0
    if direct:
        first = exp_me == 0

        def both_halves(mine, theirs):
            return jnp.concatenate(
                [jnp.where(first, mine, theirs), jnp.where(first, theirs, mine)], axis=1
            )

        own_rows = lax.dynamic_slice_in_dim(placing, exp_me * per, per, axis=0)
        res_both = both_halves(residual, res_come)
        res_all = dot(own_rows, res_both).astype(BF)
        res_all = jnp.concatenate([res_all, move(res_all, *res_masks[0])], axis=0)
        proj_near = swap_exp(proj_go)
    else:
        res_rows = dot(placing, residual).astype(BF)
        res_all = lax.all_to_all(
            res_rows.reshape(experts, per, -1), "exp", split_axis=0, concat_axis=2, tiled=True
        )[0]
        proj_all = lax.all_gather(out_proj, "exp", axis=1, tiled=True)

    all_kv = jnp.concatenate([all_kv, far_kv], axis=0)
    parts = []
    for h in range(heads):
        cols = slice(h * HD, (h + 1) * HD)
        k_h, v_h = all_kv[:, :width][:, cols], all_kv[:, width:][:, cols]
        scores = lax.dot_general(
            q_rows[:, cols], k_h, (((1,), (1,)), ((), ())), preferred_element_type=F32
        )
        scores = jnp.where(allowed, scores * (1.0 / math.sqrt(HD)), -1e30)
        top = jnp.max(scores, axis=1, keepdims=True)
        expo = jnp.where(allowed, jnp.exp(scores - top), 0.0)
        total = jnp.sum(expo, axis=1, keepdims=True)
        parts.append((dot(expo.astype(BF), v_h) / total).astype(BF))
    att = jnp.concatenate(parts, axis=1).reshape(experts, per, width)

    if direct:
        go = jnp.broadcast_to(att[None], (n // 2, experts, per, width)).reshape(-1, per, width)
        go, go_w, proj_near, res_all = lax.optimization_barrier((go, near_w, proj_near, res_all))
        proj_far = swap_core(proj_near)
        proj_come = jnp.concatenate([by_core(proj_near, proj_far), by_core(proj_far, proj_near)], axis=0)
        proj_all = both_halves(out_proj, proj_come)
        far_w = tuple(swap_core(w) for w in go_w)
        res_come = [move(res_all, *res_masks[1]), move(res_all, *res_masks[2])]
        res_come.append(move(res_come[0], *res_masks[2]))
        res_all = [part.reshape(-1, per, part.shape[1]) for part in [res_all] + res_come]
        groups = [[(2 * k + c) * experts + e for k in range(n // 2) for e in range(experts)] for c in (0, 1)]
        att_all = lax.all_to_all(
            go, ("ctx", "exp"), split_axis=0, concat_axis=0, axis_index_groups=groups, tiled=True
        )
        order = scattered(sum_stages)
        places = [gathered([[masks[c]] for masks in res_masks]) for c in (0, 1)]
        res_at = by_core(*(jnp.array([place.index(o) for o in order], jnp.int32) for place in places))
        hidden, keep, send = expert(
            (me ^ jnp.array(order, jnp.int32)) >> 1, res_at, att_all,
            res_all, proj_all, norm_gain, near_w, far_w,
        )
        summed = scatter(keep, [send[k] for k in range(3)], sum_stages)
    else:
        att_all = lax.all_to_all(att, "exp", split_axis=0, concat_axis=2, tiled=True)[0]
        hidden = (res_all.astype(F32) + dot(att_all, proj_all)).astype(BF).astype(F32)
        meansq = jnp.mean(hidden * hidden, axis=1, keepdims=True)
        normed = (hidden * lax.rsqrt(meansq + 1e-05) * norm_gain).astype(BF)
        order = scattered(sum_stages)
        far_w = tuple(swap_core(w) for w in near_w)
        found = gather(normed, sum_stages).reshape(n // 2, per, -1)
        found = jnp.stack([found[gathered(sum_stages).index(o)] for o in order]).reshape(n // 2 * per, -1)
        pieces = jnp.split(expert_rows(found, near_w, far_w), 4, axis=0)
        summed = scatter(pieces[0], [piece.astype(BF) for piece in pieces[1:]], sum_stages)
    return (hidden + summed).astype(BF)[None]


def solution(mesh):
    in_specs = (
        P("ctx", "exp"),
        P("ctx", "exp"),
        P("ctx", "exp"),
        P("ctx", "exp"),
        P(None, "exp"),
        P(),
        P("exp", None, "ctx"),
        P("exp", None, "ctx"),
        P("exp", "ctx", None),
        P("ctx", None),
        P(),
    )
    out_specs = P("exp", "ctx", None)
    return jax.shard_map(body, mesh=mesh, in_specs=in_specs, out_specs=out_specs, check_vma=False)
```

```python
import functools
import math

import jax
import jax.numpy as jnp
from jax import lax
from jax.experimental import pallas as pl
from jax.experimental.pallas import tpu as pltpu
from jax.sharding import PartitionSpec as P

HD = 128
BLK = 128
VMEM_LIMIT = 50 * 2**20
BF = jnp.bfloat16
F32 = jnp.float32


def dot(a, b):
    return jnp.dot(a, b, preferred_element_type=F32)


def distances(bits):
    out = [0]
    for bit in bits:
        out = out + [o ^ bit for o in out]
    return out


def pairs_from(bits):
    return [bits[k : k + 2] for k in range(0, len(bits), 2)]


def gathered(stages):
    out = [0]
    for bits in stages:
        out = [o ^ d for d in distances(bits) for o in out]
    return out


def scattered(stages):
    if not stages:
        return [0]
    return [d ^ o for d in distances(stages[0]) for o in scattered(stages[1:])]


def prepare_kernel(me, mask, keys, values, queries, targets, kv, q_rows, placing, allowed, *, far):
    local, width = keys.shape
    kv[:, :width] = keys[...]
    kv[:, width:] = values[...]
    target = targets[...]
    experts = far["experts"]
    per = local // experts
    row = lax.broadcasted_iota(jnp.int32, (local, local), 0)
    col = lax.broadcasted_iota(jnp.int32, (local, local), 1)
    named = lax.broadcasted_iota(jnp.int32, (experts, local), 0) == target
    before = dot(named.astype(BF), (row < col).astype(BF))
    rank = jnp.sum(jnp.where(named, before, 0.0), axis=0, keepdims=True).astype(jnp.int32)
    place = (row == target * per + rank).astype(BF)
    placing[...] = place
    q_rows[...] = dot(place, queries[...]).astype(BF)
    block = lax.broadcasted_iota(jnp.int32, allowed.shape, 1) // local
    mine = (me[0] * local) // BLK
    chosen = jnp.zeros(allowed.shape, jnp.int32)
    for b, distance in enumerate(far["distances"]):
        chosen = jnp.where(block == b, mask[mine, ((me[0] ^ distance) * local) // BLK], chosen)
    allowed[...] = chosen


def prepare(me, mask, keys, values, queries, routes, experts, order):
    local, width = keys.shape
    smem, vmem = pl.BlockSpec(memory_space=pltpu.SMEM), pl.BlockSpec(memory_space=pltpu.VMEM)
    return pl.pallas_call(
        functools.partial(prepare_kernel, far=dict(experts=experts, distances=order)),
        out_shape=(
            jax.ShapeDtypeStruct((local, 2 * width), BF),
            jax.ShapeDtypeStruct(queries.shape, BF),
            jax.ShapeDtypeStruct((local, local), BF),
            jax.ShapeDtypeStruct((1, len(order) * local), jnp.int32),
        ),
        in_specs=[smem] * 2 + [vmem] * 4,
        out_specs=[vmem] * 4,
    )(me[None], mask, keys, values, queries, routes.reshape(1, local))


def expert_rows(x, near, far):
    total = None
    for gate, up, down in (near, far):
        act = (jax.nn.silu(dot(x, gate[...])) * dot(x, up[...])).astype(BF)
        part = dot(act, down[...])
        total = part if total is None else total + part
    return total


def expert_kernel(
    att_at, res_at, att, res0, res1, res2, res3, proj, gain, gate0, up0, down0, gate1, up1, down1,
    own, keep, send, acts_out, att_rows, hidden, normed, res, gates, ups, downs, sems,
):
    blocks, per, feats = res.shape
    sources, _, width = att.shape
    sources //= blocks
    pieces = send.shape[0] + 1
    size = blocks * per // (2 * pieces)
    rows = pieces * size
    tile = math.gcd(feats, 512)
    cols = [slice(c, c + tile) for c in range(0, feats, tile)]
    moves = [
        pltpu.make_async_copy(src, dst, sems.at[i])
        for i, (src, dst) in enumerate(
            (
                (gate0, gates.at[0]), (up0, ups.at[0]),
                (gate1, gates.at[1]), (up1, ups.at[1]), (down0, downs.at[0]), (down1, downs.at[1]),
                (res0, res.at[: blocks // 4]), (res1, res.at[blocks // 4 : blocks // 2]),
                (res2, res.at[blocks // 2 : 3 * blocks // 4]), (res3, res.at[3 * blocks // 4 :]),
            )
        )
    ]
    for k in (6, 7, 8, 9, 0, 1, 2, 3, 4, 5):
        moves[k].start()
    for b in range(blocks):
        for s in range(sources):
            att_rows[b * per : (b + 1) * per, s * width : (s + 1) * width] = att[
                att_at[b] * sources + s
            ]
    for k in (6, 7, 8, 9):
        moves[k].wait()
    spans = [slice(k, k + rows) for k in range(0, blocks * per, rows)]
    for span in spans:
        squares = 0.0
        for c in cols:
            projected = dot(att_rows[span, :], proj[:, c])
            added = jnp.concatenate(
                [res[res_at[b], :, c] for b in range(span.start // per, span.stop // per)], axis=0
            )
            part = (added.astype(F32) + projected).astype(BF)
            hidden[span, c] = part
            part = part.astype(F32)
            squares = squares + jnp.sum(part * part, axis=1, keepdims=True)
        scale = lax.rsqrt(squares / feats + 1e-05)
        for c in cols:
            normed[span, c] = (hidden[span, c].astype(F32) * scale * gain[:, c]).astype(BF)
    own[...] = hidden[rows : rows + per, :].astype(F32)
    acts = []
    for side in (0, 1):
        moves[2 * side].wait()
        moves[2 * side + 1].wait()
        for span in spans:
            x = normed[span, :]
            acts.append((jax.nn.silu(dot(x, gates[side])) * dot(x, ups[side])).astype(BF))
    acts_out[0] = acts[1]
    acts_out[1] = acts[3]
    moves[4].wait()
    moves[5].wait()
    project_down(acts[0], acts[2], downs, keep, send, cols)


def project_down(first, second, downs, keep, send, cols):
    size = keep.shape[0]
    for c in cols:
        total = dot(first, downs[0, :, c]) + dot(second, downs[1, :, c])
        keep[:, c] = total[:size]
        for piece in range(send.shape[0]):
            send[piece, :, c] = total[(piece + 1) * size : (piece + 2) * size].astype(BF)


def rest_kernel(acts, down0, down1, keep, send, downs, sems):
    moves = [
        pltpu.make_async_copy(down, downs.at[side], sems.at[side])
        for side, down in enumerate((down0, down1))
    ]
    for move in moves:
        move.start()
    for move in moves:
        move.wait()
    feats = downs.shape[2]
    tile = math.gcd(feats, 512)
    cols = [slice(c, c + tile) for c in range(0, feats, tile)]
    project_down(acts[0], acts[1], downs, keep, send, cols)


def rest(acts, down0, down1):
    units, feats = down0.shape
    size = acts.shape[1] // 4
    vmem, hbm = pl.BlockSpec(memory_space=pltpu.VMEM), pl.BlockSpec(memory_space=pl.ANY)
    return pl.pallas_call(
        rest_kernel,
        out_shape=(
            jax.ShapeDtypeStruct((size, feats), F32),
            jax.ShapeDtypeStruct((3, size, feats), BF),
        ),
        in_specs=[vmem] + [hbm] * 2,
        out_specs=[vmem] * 2,
        scratch_shapes=[pltpu.VMEM((2, units, feats), BF), pltpu.SemaphoreType.DMA((2,))],
        compiler_params=pltpu.CompilerParams(vmem_limit_bytes=VMEM_LIMIT),
    )(acts, down0, down1)


def expert(att_at, res_at, att, res, proj, gain, near, far):
    quarter, per, feats = res[0].shape
    blocks = 4 * quarter
    units = near[0].shape[1]
    rows = blocks * per
    smem, vmem = pl.BlockSpec(memory_space=pltpu.SMEM), pl.BlockSpec(memory_space=pltpu.VMEM)
    hbm = pl.BlockSpec(memory_space=pl.ANY)
    return pl.pallas_call(
        expert_kernel,
        out_shape=(
            jax.ShapeDtypeStruct((per, feats), F32),
            jax.ShapeDtypeStruct((rows // 8, feats), F32),
            jax.ShapeDtypeStruct((3, rows // 8, feats), BF),
            jax.ShapeDtypeStruct((2, rows // 2, units), BF),
        ),
        in_specs=[smem] * 2 + [vmem] + [hbm] * 4 + [vmem] * 2 + [hbm] * 6,
        out_specs=[vmem] * 4,
        scratch_shapes=[
            pltpu.VMEM((rows, proj.shape[0]), BF),
            pltpu.VMEM((rows, feats), BF),
            pltpu.VMEM((rows, feats), BF),
            pltpu.VMEM((blocks, per, feats), BF),
            pltpu.VMEM((2, feats, units), BF),
            pltpu.VMEM((2, feats, units), BF),
            pltpu.VMEM((2, units, feats), BF),
            pltpu.SemaphoreType.DMA((10,)),
        ],
        compiler_params=pltpu.CompilerParams(vmem_limit_bytes=VMEM_LIMIT),
        cost_estimate=pl.CostEstimate(
            flops=12 * rows * feats * units, bytes_accessed=12 * feats * units, transcendentals=0
        ),
    )(att_at, res_at, att, *res, proj, gain[None], *near, *far)


def body(
    residual, queries, keys, values, out_proj, norm_gain, w_gate, w_up, w_down, routes, block_mask
):
    local = residual.shape[0]
    n = lax.axis_size("ctx")
    experts = lax.axis_size("exp")
    per = local // experts
    me = lax.axis_index("ctx")
    exp_me = lax.axis_index("exp")
    core = me & 1
    bits = [1 << k for k in range(1, n.bit_length() - 1)]
    kv_stages = [pair[::-1] for pair in pairs_from(bits[::-1])]
    sum_stages = pairs_from(bits)
    one, two = bits[::-1], bits[:1:-1] + bits[:2]
    res_masks = list(zip(one, two))

    def by_core(even, odd):
        return jnp.where(core == 0, even, odd)

    def move(x, even, odd=None):
        masks = (even, even if odd is None else odd)
        return lax.ppermute(x, "ctx", [(i, i ^ masks[i & 1]) for i in range(n)])

    def swap_core(x):
        return move(x, 1)

    def swap_exp(x):
        return lax.ppermute(x, "exp", [(0, 1), (1, 0)])

    def gather(x, stages):
        for bits in stages:
            x = jnp.concatenate([x] + [move(x, d) for d in distances(bits)[1:]], axis=0)
        return x

    def scatter(keep, send, stages):
        parts = 1 << len(stages[1]) if len(stages) > 1 else 1
        sums = []
        for part in reversed(range(parts)):
            total = jnp.split(keep, parts, axis=0)[part]
            for piece, distance in reversed(list(zip(send, distances(stages[0])[1:]))):
                total = total + move(jnp.split(piece, parts, axis=0)[part], distance).astype(F32)
            sums.insert(0, total)
        if parts == 1:
            return sums[0]
        return scatter(sums[0], [total.astype(BF) for total in sums[1:]], stages[1:])

    kv_order = gathered(kv_stages)
    width = keys.shape[1]
    heads = width // HD
    all_kv, q_rows, placing, allowed = prepare(
        me, block_mask, keys, values, queries, routes, experts, kv_order + [o ^ 1 for o in kv_order]
    )
    allowed = allowed > 0
    rows = out_proj.shape[0] // 2
    proj_go = lax.dynamic_slice_in_dim(out_proj, core * rows, rows, axis=0)
    all_kv = gather(all_kv, kv_stages[:1])
    if experts == 2:
        all_kv, res_come = lax.optimization_barrier((all_kv, swap_exp(residual)))
    all_kv = gather(all_kv, kv_stages[1:-1])
    last = [move(x, d) for d in distances(kv_stages[-1])[1:] for x in jnp.split(all_kv, 2, axis=0)]
    all_kv = jnp.concatenate([all_kv] + last, axis=0)
    far_kv = swap_core(all_kv)

    near_w = (w_gate[0], w_up[0], w_down[0])
    direct = experts == 2 and per % 32 == 0 and n == 16
    if direct:
        first = exp_me == 0

        def both_halves(mine, theirs):
            return jnp.concatenate(
                [jnp.where(first, mine, theirs), jnp.where(first, theirs, mine)], axis=1
            )

        own_rows = lax.dynamic_slice_in_dim(placing, exp_me * per, per, axis=0)
        res_both = both_halves(residual, res_come)
        res_all = dot(own_rows, res_both).astype(BF)
        res_all = jnp.concatenate([res_all, move(res_all, *res_masks[0])], axis=0)
        proj_near = swap_exp(proj_go)
    else:
        res_rows = dot(placing, residual).astype(BF)
        res_all = lax.all_to_all(
            res_rows.reshape(experts, per, -1), "exp", split_axis=0, concat_axis=2, tiled=True
        )[0]
        proj_all = lax.all_gather(out_proj, "exp", axis=1, tiled=True)

    all_kv = jnp.concatenate([all_kv, far_kv], axis=0)
    parts = []
    for h in range(heads):
        cols = slice(h * HD, (h + 1) * HD)
        k_h, v_h = all_kv[:, :width][:, cols], all_kv[:, width:][:, cols]
        scores = lax.dot_general(
            q_rows[:, cols], k_h, (((1,), (1,)), ((), ())), preferred_element_type=F32
        )
        scores = jnp.where(allowed, scores * (1.0 / math.sqrt(HD)), -1e30)
        top = jnp.max(scores, axis=1, keepdims=True)
        expo = jnp.where(allowed, jnp.exp(scores - top), 0.0)
        total = jnp.sum(expo, axis=1, keepdims=True)
        parts.append((dot(expo.astype(BF), v_h) / total).astype(BF))
    att = jnp.concatenate(parts, axis=1).reshape(experts, per, width)

    if direct:
        go = jnp.broadcast_to(att[None], (n // 2, experts, per, width)).reshape(-1, per, width)
        go, go_w, proj_near, res_all = lax.optimization_barrier((go, near_w, proj_near, res_all))
        proj_far = swap_core(proj_near)
        proj_come = jnp.concatenate([by_core(proj_near, proj_far), by_core(proj_far, proj_near)], axis=0)
        proj_all = both_halves(out_proj, proj_come)
        far_w = tuple(swap_core(w) for w in go_w)
        res_come = [move(res_all, *res_masks[1]), move(res_all, *res_masks[2])]
        res_come.append(move(res_come[0], *res_masks[2]))
        res_all = [part.reshape(-1, per, part.shape[1]) for part in [res_all] + res_come]
        groups = [[(2 * k + c) * experts + e for k in range(n // 2) for e in range(experts)] for c in (0, 1)]
        att_all = lax.all_to_all(
            go, ("ctx", "exp"), split_axis=0, concat_axis=0, axis_index_groups=groups, tiled=True
        )
        order = scattered(sum_stages)
        order = order[1::2] + order[::2]
        places = [gathered([[masks[c]] for masks in res_masks]) for c in (0, 1)]
        res_at = by_core(*(jnp.array([place.index(o) for o in order], jnp.int32) for place in places))
        hidden, keep, send, acts = expert(
            (me ^ jnp.array(order, jnp.int32)) >> 1, res_at, att_all,
            res_all, proj_all, norm_gain, near_w, far_w,
        )
        total = scatter(keep, [send[k] for k in range(3)], sum_stages[:1]).astype(BF)
        keep, send = rest(acts, near_w[2], far_w[2])
        summed = scatter(keep, [send[k] for k in range(3)], sum_stages[:1])
        summed = summed + move(total, sum_stages[1][0]).astype(F32)
    else:
        att_all = lax.all_to_all(att, "exp", split_axis=0, concat_axis=2, tiled=True)[0]
        hidden = (res_all.astype(F32) + dot(att_all, proj_all)).astype(BF).astype(F32)
        meansq = jnp.mean(hidden * hidden, axis=1, keepdims=True)
        normed = (hidden * lax.rsqrt(meansq + 1e-05) * norm_gain).astype(BF)
        order = scattered(sum_stages)
        far_w = tuple(swap_core(w) for w in near_w)
        found = gather(normed, sum_stages).reshape(n // 2, per, -1)
        found = jnp.stack([found[gathered(sum_stages).index(o)] for o in order]).reshape(n // 2 * per, -1)
        pieces = jnp.split(expert_rows(found, near_w, far_w), 4, axis=0)
        summed = scatter(pieces[0], [piece.astype(BF) for piece in pieces[1:]], sum_stages)
    return (hidden + summed).astype(BF)[None]


def solution(mesh):
    in_specs = (
        P("ctx", "exp"),
        P("ctx", "exp"),
        P("ctx", "exp"),
        P("ctx", "exp"),
        P(None, "exp"),
        P(),
        P("exp", None, "ctx"),
        P("exp", None, "ctx"),
        P("exp", "ctx", None),
        P("ctx", None),
        P(),
    )
    out_specs = P("exp", "ctx", None)
    return jax.shard_map(body, mesh=mesh, in_specs=in_specs, out_specs=out_specs, check_vma=False)
```
